512 devices in a mesh: shard: 64 (over x, y_lo, z), dp: 8 (over y_hi, core).
Axes of the slice: x: 4, y: 8 (y_hi: 4, y_lo: 2; y = y_hi * 2 + y_lo), z: 8, core: 2. Of those that a mesh axis runs over, the one named last changes fastest.
Arguments:
- tokens: bfloat16 [1024, 8192], P('dp', 'shard'), may hold values from -6 to 6
- frozen_up_weight: bfloat16 [8192, 32768], P('dp', 'shard'), may hold values from -0.0625 to 0.0625
- adapter_down_factor: bfloat16 [8192, 256], P('shard'), may hold values from -0.0625 to 0.0625
- adapter_up_factor: bfloat16 [256, 32768], P(None, 'shard'), may hold values from -0.375 to 0.375
- cotangent: bfloat16 [1024, 32768], P('dp', 'shard'), may hold values from -0.59765625 to 0.59765625
- previous_task_directions: bfloat16 [8192, 1024], P('shard'), may hold values from -0.0625 to 0.0625
Outputs:
- projection_output: bfloat16 [1024, 32768], P('dp', 'shard')
- token_input_gradient: bfloat16 [1024, 8192], P('dp', 'shard')
- grad_down: float32 [8192, 256], P('shard')
- grad_up: float32 [256, 32768], P(None, 'shard')
The draws below stay inside these ranges and needn't reach their ends.
All inputs are finite; a program needn't handle non-finite values.
Results may differ from the reference program's by a relative error of at most 0.005.
Values may be sent and summed in bfloat16 or wider, within the bound.
No kernel may reach another device: no remote copies, remote signals or barrier semaphores. Data moves between devices by JAX's collectives and lax.ppermute only.
A program may use at most 64 MiB of HBM per device.

```python
import jax
import jax.numpy as jnp
from jax import lax

MODEL_WIDTH = 8192
HIDDEN_UNITS = 32768
ADAPTER_RANK = 256
K = 1024
TOKENS = 1024


def levels(own_key, dims, cuts, low, high):
    level, own = 1.0, jax.random.fold_in(own_key, 6)
    for dim, blocks in cuts:
        steps = jnp.exp(jax.random.uniform(jax.random.fold_in(own, dim), (blocks,), jnp.float32, low / len(cuts), high / len(cuts)))
        level = level * jnp.repeat(steps, dims[dim] // blocks).reshape([-1 if axis == dim else 1 for axis in range(len(dims))])
    return level


def scatter_about(key, extent, width, limit, shards=(), dtype=jnp.bfloat16):
    loudness = levels(key, extent, shards, -0.22, 0.18) if shards else 1.0
    values = jax.random.normal(key, extent, jnp.float32) * width * loudness
    return jnp.minimum(jnp.maximum(values, -limit), limit).astype(dtype)


def setup_inputs(seed: int = 0) -> dict:
    key_of = jax.random.split(jax.random.key(seed), 7)
    tokens = scatter_about(key_of[0], (TOKENS, MODEL_WIDTH), 1.0, 6.0, ((0, 8), (1, 64)))
    frozen_up_weight = scatter_about(key_of[1], (MODEL_WIDTH, HIDDEN_UNITS), MODEL_WIDTH ** -0.5, 0.0625, ((0, 8), (1, 64)))
    adapter_down_factor = scatter_about(key_of[2], (MODEL_WIDTH, ADAPTER_RANK), MODEL_WIDTH ** -0.5, 0.0625, ((0, 64),))
    adapter_up_factor = scatter_about(key_of[3], (ADAPTER_RANK, HIDDEN_UNITS), ADAPTER_RANK ** -0.5, 0.375, ((1, 64),))
    cotangent = scatter_about(key_of[4], (TOKENS, HIDDEN_UNITS), 0.1, 0.59765625, ((0, 8), (1, 64)))
    previous_task_directions = scatter_about(key_of[5], (MODEL_WIDTH, K), MODEL_WIDTH ** -0.5, 0.0625, ((0, 64),))
    return {"tokens": tokens, "frozen_up_weight": frozen_up_weight, "adapter_down_factor": adapter_down_factor, "adapter_up_factor": adapter_up_factor, "cotangent": cotangent, "previous_task_directions": previous_task_directions}


def reference(tokens, frozen_up_weight, adapter_down_factor, adapter_up_factor, cotangent, previous_task_directions):
    lowrank_activation = jnp.dot(tokens, adapter_down_factor, preferred_element_type=jnp.float32).astype(jnp.bfloat16)
    projection_output = (jnp.dot(tokens, frozen_up_weight, preferred_element_type=jnp.float32)
                 + jnp.dot(lowrank_activation, adapter_up_factor, preferred_element_type=jnp.float32)).astype(jnp.bfloat16)
    backward_lowrank = jnp.dot(cotangent, adapter_up_factor.T, preferred_element_type=jnp.float32).astype(jnp.bfloat16)
    token_input_gradient = (jnp.dot(cotangent, frozen_up_weight.T, preferred_element_type=jnp.float32)
                  + jnp.dot(backward_lowrank, adapter_down_factor.T, preferred_element_type=jnp.float32)).astype(jnp.bfloat16)
    grad_up = jnp.dot(lowrank_activation.T, cotangent, preferred_element_type=jnp.float32)
    raw_grad = jnp.dot(tokens.T, backward_lowrank, preferred_element_type=jnp.float32)
    basis_wide = previous_task_directions.astype(jnp.float32)
    coefficients = jnp.dot(basis_wide.T, raw_grad, precision=lax.Precision.HIGHEST)
    grad_down = raw_grad - jnp.dot(basis_wide, coefficients, precision=lax.Precision.HIGHEST)
    return projection_output, token_input_gradient, grad_down, grad_up
```

```python
import jax
import jax.numpy as jnp
from jax import lax
from jax.sharding import PartitionSpec as P

F32 = jnp.float32
BF16 = jnp.bfloat16


def dot(left, right, contract):
    return lax.dot_general(left, right, ((contract[0], contract[1]), ((), ())), preferred_element_type=F32)


def exchange(pieces, axis):
    return lax.all_to_all(pieces, axis, split_axis=0, concat_axis=0, tiled=True)


def to_all(block, count):
    return jnp.broadcast_to(block[None], (count, *block.shape))


def local(tokens, weight, down, up, cotangent, directions):
    shards = lax.axis_size("shard")
    groups = lax.axis_size("dp")
    batch, block = tokens.shape
    rank = down.shape[1]
    past = directions.shape[1]

    weight_full = lax.all_gather(weight, "dp", axis=0, tiled=True)

    share = jnp.concatenate(
        [
            dot(down, tokens, ((0,), (1,))),
            dot(directions, tokens, ((0,), (1,))),
            dot(up, cotangent, ((1,), (1,))),
        ],
        axis=0,
    ).astype(BF16)
    rows = share.shape[0] // shards
    first = exchange(
        jnp.concatenate([to_all(tokens, shards), share.reshape(shards, rows, batch)], axis=1), "shard"
    )
    tokens_full = first[:, :batch]
    summed = jnp.sum(first[:, batch:].astype(F32), axis=0).astype(BF16)

    partial_gradient = dot(weight_full, cotangent, ((1,), (1,))).astype(BF16)
    second = exchange(
        jnp.concatenate(
            [partial_gradient.reshape(shards, block, batch), to_all(summed, shards)], axis=1
        ),
        "shard",
    )
    gradient = jnp.sum(second[:, :block].astype(F32), axis=0)
    whole = second[:, block:].reshape(shards * rows, batch)
    low, along, back_low = whole[:rank], whole[rank : rank + past], whole[rank + past :]

    frozen = dot(tokens_full.transpose(1, 0, 2).reshape(batch, shards * block), weight_full, ((1,), (0,)))
    projection_output = (frozen + dot(low, up, ((0,), (0,)))).astype(BF16)
    token_input_gradient = (gradient + dot(down, back_low, ((1,), (0,)))).T.astype(BF16)

    up_part = dot(cotangent, low, ((0,), (1,)))
    kept = tokens.astype(F32).T - dot(directions, along, ((1,), (0,)))
    kept_high = kept.astype(BF16)
    kept_rest = (kept - kept_high.astype(F32)).astype(BF16)
    down_part = dot(kept_high, back_low, ((1,), (1,))) + dot(kept_rest, back_low, ((1,), (1,)))
    up_rows, down_rows = up_part.shape[0] // groups, block // groups
    third = exchange(
        jnp.concatenate(
            [up_part.reshape(groups, up_rows, rank), down_part.reshape(groups, down_rows, rank)], axis=1
        ).astype(BF16),
        "dp",
    )
    mine = jnp.sum(third.astype(F32), axis=0).astype(BF16)
    fourth = exchange(to_all(mine, groups), "dp").astype(F32)
    grad_up = fourth[:, :up_rows].reshape(groups * up_rows, rank).T
    grad_down = fourth[:, up_rows:].reshape(block, rank)
    return projection_output, token_input_gradient, grad_down, grad_up


def solution(mesh):
    placed = (
        P("dp", "shard"),
        P("dp", "shard"),
        P("shard", None),
        P(None, "shard"),
        P("dp", "shard"),
        P("shard", None),
    )
    return jax.shard_map(
        local,
        mesh=mesh,
        in_specs=placed,
        out_specs=(P("dp", "shard"), P("dp", "shard"), P("shard", None), P(None, "shard")),
        check_vma=False,
    )
```

```python
import jax
import jax.numpy as jnp
from jax import lax
from jax.sharding import Mesh
from jax.sharding import PartitionSpec as P

F32 = jnp.float32
BF16 = jnp.bfloat16
AXES = ("x", "ylo", "z", "yhi", "core")
SIZES = (4, 2, 8, 4, 2)
SHARD = ("x", "ylo", "z")
DP = ("yhi", "core")
THERE = [
    ((x * 2 + l) * 4 + h, ((2 * (h // 2) + l) * 2 + h % 2) * 4 + x)
    for x in range(4)
    for l in range(2)
    for h in range(4)
]
BACK = [(b, a) for a, b in THERE]
HOME = [
    [(l * 4 + h, ((h ^ j) % 2) * 4 + (h ^ j) // 2 * 2 + l) for l in range(2) for h in range(4)] for j in range(4)
]


SPREAD = [
    [(l * 4 + h, (h % 2) * 4 + ((h // 2 * 2 + l) ^ j)) for l in range(2) for h in range(4)] for j in range(4)
]


def dot(left, right, contract):
    return lax.dot_general(left, right, ((contract[0], contract[1]), ((), ())), preferred_element_type=F32)


def exchange(pieces, axes):
    return lax.all_to_all(pieces, axes, split_axis=0, concat_axis=0, tiled=True)


def to_all(block, axes):
    return jnp.broadcast_to(block[None], (lax.axis_size(axes), *block.shape))


def add_up(pieces):
    return jnp.sum(pieces.astype(F32), axis=0)


def trade(block, axis):
    return lax.ppermute(block, axis, [(0, 1), (1, 0)])


def local(tokens, weight, down, up, cotangent, directions):
    n_z = lax.axis_size("z")
    batch, block = tokens.shape
    rank = down.shape[1]
    past = directions.shape[1]
    depth, hidden = weight.shape

    weights = lax.all_gather(weight, ("ylo", "core"), axis=0, tiled=True).reshape(2, 2 * depth, hidden)
    moved = lax.ppermute(tokens, ("x", "ylo", "yhi"), THERE)
    high = lax.axis_index("yhi")
    arrived = jnp.stack([lax.ppermute(cotangent, ("ylo", "yhi"), SPREAD[j]) for j in range(4)])
    cotangents = [lax.dynamic_index_in_dim(arrived, high ^ p, 0, keepdims=False) for p in range(4)]

    share = jnp.concatenate(
        [
            dot(down, tokens, ((0,), (1,))),
            dot(directions, tokens, ((0,), (1,))),
            dot(up, cotangent, ((1,), (1,))),
        ],
        axis=0,
    ).astype(BF16)
    first = exchange(
        jnp.concatenate([to_all(moved, ("x", "z")), share.reshape(4 * n_z, -1, batch)], axis=1), ("x", "z")
    )
    summed = add_up(first[:, batch:])
    summed = (summed + trade(summed, "ylo")).astype(BF16)
    later, summed = lax.optimization_barrier((cotangent, summed))
    cotangent_column = lax.all_gather(later, DP, axis=0, tiled=True)

    panel = first[:, :batch].reshape(2, 2 * n_z, batch, block).transpose(0, 2, 1, 3)
    panel = panel.reshape(2 * batch, 2 * n_z * block)
    frozen = [dot(panel, weights[i], ((1,), (0,))).astype(BF16).reshape(2, batch, hidden) for i in range(2)]
    frozen = jnp.stack(frozen, axis=1).reshape(4, batch, hidden)
    frozen = sum(
        lax.ppermute(
            lax.dynamic_index_in_dim(frozen, lax.axis_index("yhi") ^ j, 0, keepdims=False), ("ylo", "yhi"), HOME[j]
        ).astype(F32)
        for j in range(4)
    )

    slabs = [
        (
            dot(weights[0], cotangents[2 * i], ((1,), (1,))) + dot(weights[1], cotangents[2 * i + 1], ((1,), (1,)))
        ).astype(BF16)
        for i in range(2)
    ]
    slabs = jnp.concatenate(slabs).reshape(4 * n_z, block, batch)
    second = exchange(jnp.concatenate([slabs, to_all(summed, ("x", "z"))], axis=1), ("x", "z"))
    second, frozen = lax.optimization_barrier((second, frozen))
    gradient = lax.ppermute(add_up(second[:, :block]), ("x", "ylo", "yhi"), BACK)
    whole = second[:, block:].reshape(share.shape)
    low, along, back_low = whole[:rank], whole[rank : rank + past], whole[rank + past :]

    projection_output = (frozen + dot(low, up, ((0,), (0,)))).astype(BF16)
    token_input_gradient = (gradient + dot(down, back_low, ((1,), (0,)))).T.astype(BF16)

    kept = tokens.astype(F32).T - dot(directions, along, ((1,), (0,)))
    kept_high = kept.astype(BF16)
    kept_rest = (kept - kept_high.astype(F32)).astype(BF16)
    down_part = dot(back_low, kept_high, ((1,), (1,))) + dot(back_low, kept_rest, ((1,), (1,)))
    pair = exchange(to_all(jnp.concatenate([low, down_part.astype(BF16)], axis=0), "yhi"), "yhi")
    lows = pair[:, :rank]
    down_sum = add_up(pair[:, rank:])
    lows_beside, down_beside = trade(lows, "core"), trade(down_sum, "core")
    grad_down = (down_sum + down_beside).T
    first_core = lax.axis_index("core") == 0
    both = jnp.stack([jnp.where(first_core, lows, lows_beside), jnp.where(first_core, lows_beside, lows)], axis=1)
    low_column = both.transpose(2, 0, 1, 3).reshape(rank, 8 * batch)
    grad_up = dot(low_column, cotangent_column, ((1,), (0,)))
    return projection_output, token_input_gradient, grad_down, grad_up


def solution(mesh):
    fine = Mesh(mesh.devices.reshape(SIZES), AXES)
    placed = (P(DP, SHARD), P(DP, SHARD), P(SHARD, None), P(None, SHARD), P(DP, SHARD), P(SHARD, None))
    return jax.shard_map(
        local,
        mesh=fine,
        in_specs=placed,
        out_specs=(P(DP, SHARD), P(DP, SHARD), P(SHARD, None), P(None, SHARD)),
        check_vma=False,
    )
```

```python
import jax
import jax.numpy as jnp
from jax import lax
from jax.experimental import pallas as pl
from jax.experimental.pallas import tpu as pltpu
from jax.sharding import Mesh
from jax.sharding import PartitionSpec as P

F32 = jnp.float32
BF16 = jnp.bfloat16
AXES = ("x", "ylo", "z", "yhi", "core")
SIZES = (4, 2, 8, 4, 2)
SHARD = ("x", "ylo", "z")
DP = ("yhi", "core")
THERE = [
    ((x * 2 + l) * 4 + h, ((2 * (h // 2) + l) * 2 + h % 2) * 4 + x)
    for x in range(4)
    for l in range(2)
    for h in range(4)
]
BACK = [(b, a) for a, b in THERE]
HOME = [
    [(l * 4 + h, ((h ^ j) % 2) * 4 + (h ^ j) // 2 * 2 + l) for l in range(2) for h in range(4)] for j in range(4)
]


def dot(left, right, contract):
    return lax.dot_general(left, right, ((contract[0], contract[1]), ((), ())), preferred_element_type=F32)


def exchange(pieces, axes):
    return lax.all_to_all(pieces, axes, split_axis=0, concat_axis=0, tiled=True)


def to_all(block, axes):
    return jnp.broadcast_to(block[None], (lax.axis_size(axes), *block.shape))


def add_up(pieces):
    return jnp.sum(pieces.astype(F32), axis=0)


def trade(block, axis):
    return lax.ppermute(block, axis, [(0, 1), (1, 0)])


def slab_kernel(core_ref, near_ref, far_ref, near_beside_ref, far_beside_ref, own_ref, other_ref, out_ref):
    block = batch = out_ref.shape[4]

    def write(own_weight, other_weight):
        total = lax.dot_general(own_weight, own_ref[...], (((1,), (1,)), ((), ())), preferred_element_type=F32)
        total += lax.dot_general(other_weight, other_ref[...], (((1,), (1,)), ((), ())), preferred_element_type=F32)
        total = total.astype(BF16)
        for i in range(2):
            for j in range(out_ref.shape[2]):
                out_ref[i, 0, j, :block, :] = total[j * block : (j + 1) * block, i * batch : (i + 1) * batch]

    @pl.when(pl.program_id(0) == 0)
    def _():
        write(near_ref[...], far_ref[...])

    @pl.when(pl.program_id(0) == 1)
    def _():
        write(near_beside_ref[...], far_beside_ref[...])


def slabs_of(core, own_core, other_core, own, other, extra):
    batch = own.shape[0] // 2
    block, take = batch, 4
    depth, hidden = own_core[0].shape
    steps = depth // (take * block)
    early = pl.BlockSpec((take * block, hidden), lambda s, r, _: (jnp.where(s == 0, r, steps - 1), 0))
    late = pl.BlockSpec((take * block, hidden), lambda s, r, _: (jnp.where(s == 0, 0, r), 0))
    whole = pl.BlockSpec(own.shape, lambda s, r, _: (0, 0))
    out = pl.pallas_call(
        slab_kernel,
        grid_spec=pltpu.PrefetchScalarGridSpec(
            num_scalar_prefetch=1,
            grid=(2, steps),
            in_specs=[early, early, late, late, whole, whole],
            out_specs=pl.BlockSpec(
                (2, 1, take, block + extra, batch), lambda s, r, c: (0, s ^ c[0], r, 0, 0)
            ),
        ),
        out_shape=jax.ShapeDtypeStruct((2, 2, steps * take, block + extra, batch), BF16),
        cost_estimate=pl.CostEstimate(
            flops=16 * depth * hidden * batch, bytes_accessed=8 * depth * hidden, transcendentals=0
        ),
    )(core[None], *own_core, *other_core, own, other)
    return out.reshape(4 * steps * take, block + extra, batch)


def local(tokens, weight, down, up, cotangent, directions):
    n_z = lax.axis_size("z")
    batch, block = tokens.shape
    rank = down.shape[1]
    past = directions.shape[1]
    depth, hidden = weight.shape

    ylo, high, core = (lax.axis_index(a) for a in ("ylo", "yhi", "core"))
    columns = lax.all_gather(cotangent, ("yhi", "ylo"), axis=0).reshape(2, 2, 2, batch, hidden)
    moved = lax.ppermute(tokens, ("x", "ylo", "yhi"), THERE)

    share = jnp.concatenate(
        [
            dot(down, tokens, ((0,), (1,))),
            dot(directions, tokens, ((0,), (1,))),
            dot(up, cotangent, ((1,), (1,))),
        ],
        axis=0,
    ).astype(BF16)
    first = jnp.concatenate([to_all(moved, ("x", "z")), share.reshape(4 * n_z, -1, batch)], axis=1)
    first, weight = lax.optimization_barrier((first, weight))
    first = exchange(first, ("x", "z"))

    far = trade(weight, "ylo")
    own_core, other_core = (weight, far), (trade(weight, "core"), trade(far, "core"))
    own, other = (
        lax.dynamic_slice(columns, (0, ylo, l, 0, 0), (2, 1, 1, batch, hidden)).reshape(2 * batch, hidden)
        for l in (ylo, 1 - ylo)
    )
    cotangent_column = lax.dynamic_index_in_dim(columns, ylo, 2, keepdims=False).reshape(4 * batch, hidden)
    first, own_core, other_core, own, other = lax.optimization_barrier((first, own_core, other_core, own, other))
    summed = add_up(first[:, batch:])
    beside = trade(summed, "ylo")
    panels = first[:, :batch].reshape(2, 2, n_z, batch, block)
    panels = [
        lax.dynamic_index_in_dim(panels, c, 1, keepdims=False).transpose(0, 2, 1, 3).reshape(2 * batch, depth)
        for c in (core, 1 - core)
    ]
    frozen = [
        (dot(panels[0], own_core[i], ((1,), (0,))) + dot(panels[1], other_core[i], ((1,), (0,)))).astype(BF16)
        for i in range(2)
    ]
    frozen = jnp.stack([f.reshape(2, batch, hidden) for f in frozen], axis=1).reshape(4, batch, hidden)
    frozen = sum(
        lax.ppermute(
            lax.dynamic_index_in_dim(frozen, high ^ j ^ ylo, 0, keepdims=False), ("ylo", "yhi"), HOME[j]
        ).astype(F32)
        for j in range(4)
    )

    slabs = slabs_of(core, own_core, other_core, own, other, summed.shape[0])
    slabs, beside = lax.optimization_barrier((slabs, beside))
    summed = (summed + beside).astype(BF16)
    second = exchange(
        lax.dynamic_update_slice(slabs, to_all(summed, ("x", "z")), (0, block, 0)), ("x", "z")
    )
    second, frozen = lax.optimization_barrier((second, frozen))
    gradient = lax.ppermute(add_up(second[:, :block]), ("x", "ylo", "yhi"), BACK)
    whole = second[:, block:].reshape(share.shape)
    low, along, back_low = whole[:rank], whole[rank : rank + past], whole[rank + past :]

    projection_output = (frozen + dot(low, up, ((0,), (0,)))).astype(BF16)
    token_input_gradient = (gradient + dot(down, back_low, ((1,), (0,)))).T.astype(BF16)

    kept = tokens.astype(F32).T - dot(directions, along, ((1,), (0,)))
    kept_high = kept.astype(BF16)
    kept_rest = (kept - kept_high.astype(F32)).astype(BF16)
    down_part = dot(back_low, kept_high, ((1,), (1,))) + dot(back_low, kept_rest, ((1,), (1,)))
    pair = exchange(to_all(jnp.concatenate([low, down_part.astype(BF16)], axis=0), "yhi"), "yhi")
    low_column = pair[:, :rank].transpose(1, 0, 2).reshape(rank, 4 * batch)
    up_part = dot(low_column, cotangent_column, ((1,), (0,)))
    grad_up = up_part + trade(up_part, "core")
    down_part = add_up(pair[:, rank:])
    grad_down = (down_part + trade(down_part, "core")).T
    return projection_output, token_input_gradient, grad_down, grad_up


def solution(mesh):
    fine = Mesh(mesh.devices.reshape(SIZES), AXES)
    placed = (P(DP, SHARD), P(DP, SHARD), P(SHARD, None), P(None, SHARD), P(DP, SHARD), P(SHARD, None))
    return jax.shard_map(
        local,
        mesh=fine,
        in_specs=placed,
        out_specs=(P(DP, SHARD), P(DP, SHARD), P(SHARD, None), P(None, SHARD)),
        check_vma=False,
    )
```

```python
import jax
import jax.numpy as jnp
from jax import lax
from jax.experimental import pallas as pl
from jax.experimental.pallas import tpu as pltpu
from jax.sharding import Mesh
from jax.sharding import PartitionSpec as P

F32 = jnp.float32
BF16 = jnp.bfloat16
AXES = ("x", "ylo", "z", "yhi", "core")
SIZES = (4, 2, 8, 4, 2)
SHARD = ("x", "ylo", "z")
DP = ("yhi", "core")
THERE = [
    ((x * 2 + l) * 4 + h, ((2 * (h // 2) + l) * 2 + h % 2) * 4 + x)
    for x in range(4)
    for l in range(2)
    for h in range(4)
]
BACK = [(b, a) for a, b in THERE]
HOME = [
    [(l * 4 + h, ((h ^ j) % 2) * 4 + (h ^ j) // 2 * 2 + l) for l in range(2) for h in range(4)] for j in range(4)
]


SPREAD = [
    [(l * 4 + h, (h % 2) * 4 + ((h // 2 * 2 + l) ^ j)) for l in range(2) for h in range(4)] for j in range(4)
]


def dot(left, right, contract):
    return lax.dot_general(left, right, ((contract[0], contract[1]), ((), ())), preferred_element_type=F32)


def exchange(pieces, axes):
    return lax.all_to_all(pieces, axes, split_axis=0, concat_axis=0, tiled=True)


def to_all(block, axes):
    return jnp.broadcast_to(block[None], (lax.axis_size(axes), *block.shape))


def add_up(pieces):
    return jnp.sum(pieces.astype(F32), axis=0)


def trade(block, axis):
    return lax.ppermute(block, axis, [(0, 1), (1, 0)])


def slab_kernel(where_ref, near_ref, far_ref, near_beside_ref, far_beside_ref, arrived_ref, out_ref):
    first = where_ref[1]
    block = batch = out_ref.shape[4]

    def write(own_weight, other_weight):
        total = None
        for l, weight in enumerate((own_weight, other_weight)):
            right = jnp.concatenate([arrived_ref[first ^ l], arrived_ref[first ^ l ^ 2]], axis=0)
            part = lax.dot_general(weight, right, (((1,), (1,)), ((), ())), preferred_element_type=F32)
            total = part if total is None else total + part
        total = total.astype(BF16)
        for i in range(2):
            for j in range(out_ref.shape[2]):
                out_ref[i, 0, j, :block, :] = total[j * block : (j + 1) * block, i * batch : (i + 1) * batch]

    @pl.when(pl.program_id(0) == 0)
    def _():
        write(near_ref[...], far_ref[...])

    @pl.when(pl.program_id(0) == 1)
    def _():
        write(near_beside_ref[...], far_beside_ref[...])


def slabs_of(core, first, own_core, other_core, arrived, extra):
    batch = arrived.shape[1]
    block, take = batch, 4
    depth, hidden = own_core[0].shape
    steps = depth // (take * block)
    early = pl.BlockSpec((take * block, hidden), lambda s, r, _: (jnp.where(s == 0, r, steps - 1), 0))
    late = pl.BlockSpec((take * block, hidden), lambda s, r, _: (jnp.where(s == 0, 0, r), 0))
    whole = pl.BlockSpec(arrived.shape, lambda s, r, _: (0, 0, 0))
    out = pl.pallas_call(
        slab_kernel,
        grid_spec=pltpu.PrefetchScalarGridSpec(
            num_scalar_prefetch=1,
            grid=(2, steps),
            in_specs=[early, early, late, late, whole],
            out_specs=pl.BlockSpec(
                (2, 1, take, block + extra, batch), lambda s, r, c: (0, s ^ c[0], r, 0, 0)
            ),
        ),
        out_shape=jax.ShapeDtypeStruct((2, 2, steps * take, block + extra, batch), BF16),
        cost_estimate=pl.CostEstimate(
            flops=16 * depth * hidden * batch, bytes_accessed=8 * depth * hidden, transcendentals=0
        ),
    )(jnp.stack([core, first]), *own_core, *other_core, arrived)
    return out.reshape(4 * steps * take, block + extra, batch)


def local(tokens, weight, down, up, cotangent, directions):
    n_z = lax.axis_size("z")
    batch, block = tokens.shape
    rank = down.shape[1]
    past = directions.shape[1]
    depth, hidden = weight.shape

    ylo, high, core = (lax.axis_index(a) for a in ("ylo", "yhi", "core"))
    moved = lax.ppermute(tokens, ("x", "ylo", "yhi"), THERE)

    share = jnp.concatenate(
        [
            dot(down, tokens, ((0,), (1,))),
            dot(directions, tokens, ((0,), (1,))),
            dot(up, cotangent, ((1,), (1,))),
        ],
        axis=0,
    ).astype(BF16)
    first = jnp.concatenate([to_all(moved, ("x", "z")), share.reshape(4 * n_z, -1, batch)], axis=1)
    first, weight, later = lax.optimization_barrier((first, weight, cotangent))
    first = exchange(first, ("x", "z"))

    far = trade(weight, "ylo")
    own_core, other_core = (weight, far), (trade(weight, "core"), trade(far, "core"))
    arrived = jnp.stack([lax.ppermute(later, ("ylo", "yhi"), SPREAD[j]) for j in range(4)])
    first, own_core, other_core, arrived = lax.optimization_barrier((first, own_core, other_core, arrived))
    summed = add_up(first[:, batch:])
    beside = trade(summed, "ylo")
    panels = first[:, :batch].reshape(2, 2, n_z, batch, block)
    panels = [
        lax.dynamic_index_in_dim(panels, c, 1, keepdims=False).transpose(0, 2, 1, 3).reshape(2 * batch, depth)
        for c in (core, 1 - core)
    ]
    frozen = [
        (dot(panels[0], own_core[i], ((1,), (0,))) + dot(panels[1], other_core[i], ((1,), (0,)))).astype(BF16)
        for i in range(2)
    ]
    frozen = jnp.stack([f.reshape(2, batch, hidden) for f in frozen], axis=1).reshape(4, batch, hidden)
    frozen = sum(
        lax.ppermute(
            lax.dynamic_index_in_dim(frozen, high ^ j ^ ylo, 0, keepdims=False), ("ylo", "yhi"), HOME[j]
        ).astype(F32)
        for j in range(4)
    )

    slabs = slabs_of(core, high ^ ylo, own_core, other_core, arrived, summed.shape[0])
    slabs, beside = lax.optimization_barrier((slabs, beside))
    summed = (summed + beside).astype(BF16)
    second = exchange(
        lax.dynamic_update_slice(slabs, to_all(summed, ("x", "z")), (0, block, 0)), ("x", "z")
    )
    kept = [lax.dynamic_index_in_dim(arrived, high ^ ylo ^ p, 0, keepdims=False) for p in (0, 2, 1, 3)]
    column = jnp.concatenate([*kept[:2], trade(jnp.concatenate(kept[2:]), "ylo")])
    second, frozen, column = lax.optimization_barrier((second, frozen, column))
    gradient = lax.ppermute(add_up(second[:, :block]), ("x", "ylo", "yhi"), BACK)
    whole = second[:, block:].reshape(share.shape)
    low, along, back_low = whole[:rank], whole[rank : rank + past], whole[rank + past :]

    projection_output = (frozen + dot(low, up, ((0,), (0,)))).astype(BF16)
    token_input_gradient = (gradient + dot(down, back_low, ((1,), (0,)))).T.astype(BF16)

    kept = tokens.astype(F32).T - dot(directions, along, ((1,), (0,)))
    kept_high = kept.astype(BF16)
    kept_rest = (kept - kept_high.astype(F32)).astype(BF16)
    down_part = dot(back_low, kept_high, ((1,), (1,))) + dot(back_low, kept_rest, ((1,), (1,)))
    pair = exchange(to_all(jnp.concatenate([low, down_part.astype(BF16)], axis=0), "yhi"), "yhi")
    lows = pair[:, :rank].reshape(2, 2, rank, batch)
    lows = [lax.dynamic_index_in_dim(lows, l, 1, keepdims=False) for l in (ylo, 1 - ylo)]
    up_part = dot(jnp.concatenate([*lows[0], *lows[1]], axis=1), column, ((1,), (0,)))
    ours = jnp.concatenate([up_part, add_up(pair[:, rank:])], axis=1)
    ours = ours + trade(ours.astype(BF16), "core").astype(F32)
    grad_up, grad_down = ours[:, :hidden], ours[:, hidden:].T
    return projection_output, token_input_gradient, grad_down, grad_up


def solution(mesh):
    fine = Mesh(mesh.devices.reshape(SIZES), AXES)
    placed = (P(DP, SHARD), P(DP, SHARD), P(SHARD, None), P(None, SHARD), P(DP, SHARD), P(SHARD, None))
    return jax.shard_map(
        local,
        mesh=fine,
        in_specs=placed,
        out_specs=(P(DP, SHARD), P(DP, SHARD), P(SHARD, None), P(None, SHARD)),
        check_vma=False,
    )
```

```python
import jax
import jax.numpy as jnp
from jax import lax
from jax.experimental import pallas as pl
from jax.experimental.pallas import tpu as pltpu
from jax.sharding import Mesh
from jax.sharding import PartitionSpec as P

F32 = jnp.float32
BF16 = jnp.bfloat16
AXES = ("x", "ylo", "z", "yhi", "core")
SIZES = (4, 2, 8, 4, 2)
SHARD = ("x", "ylo", "z")
DP = ("yhi", "core")
THERE = [
    ((x * 2 + l) * 4 + h, ((2 * (h // 2) + l) * 2 + h % 2) * 4 + x)
    for x in range(4)
    for l in range(2)
    for h in range(4)
]
BACK = [(b, a) for a, b in THERE]
HOME = [
    [(l * 4 + h, ((h ^ j) % 2) * 4 + (h ^ j) // 2 * 2 + l) for l in range(2) for h in range(4)] for j in range(4)
]


SPREAD = [
    [(l * 4 + h, (h % 2) * 4 + ((h // 2 * 2 + l) ^ j)) for l in range(2) for h in range(4)] for j in range(4)
]


def dot(left, right, contract):
    return lax.dot_general(left, right, ((contract[0], contract[1]), ((), ())), preferred_element_type=F32)


def exchange(pieces, axes):
    return lax.all_to_all(pieces, axes, split_axis=0, concat_axis=0, tiled=True)


def to_all(block, axes):
    return jnp.broadcast_to(block[None], (lax.axis_size(axes), *block.shape))


def add_up(pieces):
    return jnp.sum(pieces.astype(F32), axis=0)


def trade(block, axis):
    return lax.ppermute(block, axis, [(0, 1), (1, 0)])


def slab_kernel(where_ref, near_ref, far_ref, near_beside_ref, far_beside_ref, arrived_ref, out_ref):
    first = where_ref[1]
    block = batch = out_ref.shape[4]

    def write(own_weight, other_weight):
        total = None
        for l, weight in enumerate((own_weight, other_weight)):
            right = jnp.concatenate([arrived_ref[first ^ l], arrived_ref[first ^ l ^ 2]], axis=0)
            part = lax.dot_general(weight, right, (((1,), (1,)), ((), ())), preferred_element_type=F32)
            total = part if total is None else total + part
        total = total.astype(BF16)
        for i in range(2):
            for j in range(out_ref.shape[2]):
                out_ref[i, 0, j, :block, :] = total[j * block : (j + 1) * block, i * batch : (i + 1) * batch]

    @pl.when(pl.program_id(0) == 0)
    def _():
        write(near_ref[...], far_ref[...])

    @pl.when(pl.program_id(0) == 1)
    def _():
        write(near_beside_ref[...], far_beside_ref[...])


def slabs_of(core, first, own_core, other_core, arrived, extra):
    batch = arrived.shape[1]
    block, take = batch, 4
    depth, hidden = own_core[0].shape
    steps = depth // (take * block)
    early = pl.BlockSpec((take * block, hidden), lambda s, r, _: (jnp.where(s == 0, r, steps - 1), 0))
    late = pl.BlockSpec((take * block, hidden), lambda s, r, _: (jnp.where(s == 0, 0, r), 0))
    whole = pl.BlockSpec(arrived.shape, lambda s, r, _: (0, 0, 0))
    out = pl.pallas_call(
        slab_kernel,
        grid_spec=pltpu.PrefetchScalarGridSpec(
            num_scalar_prefetch=1,
            grid=(2, steps),
            in_specs=[early, early, late, late, whole],
            out_specs=pl.BlockSpec(
                (2, 1, take, block + extra, batch), lambda s, r, c: (0, s ^ c[0], r, 0, 0)
            ),
        ),
        out_shape=jax.ShapeDtypeStruct((2, 2, steps * take, block + extra, batch), BF16),
        cost_estimate=pl.CostEstimate(
            flops=16 * depth * hidden * batch, bytes_accessed=8 * depth * hidden, transcendentals=0
        ),
    )(jnp.stack([core, first]), *own_core, *other_core, arrived)
    return out.reshape(4 * steps * take, block + extra, batch)


def local(tokens, weight, down, up, cotangent, directions):
    n_z = lax.axis_size("z")
    batch, block = tokens.shape
    rank = down.shape[1]
    past = directions.shape[1]
    depth, hidden = weight.shape

    ylo, high, core = (lax.axis_index(a) for a in ("ylo", "yhi", "core"))
    moved = lax.ppermute(tokens, ("x", "ylo", "yhi"), THERE)

    share = jnp.concatenate(
        [
            dot(down, tokens, ((0,), (1,))),
            dot(directions, tokens, ((0,), (1,))),
            dot(up, cotangent, ((1,), (1,))),
        ],
        axis=0,
    ).astype(BF16)
    first = jnp.concatenate([to_all(moved, ("x", "z")), share.reshape(4 * n_z, -1, batch)], axis=1)
    first, weight, later = lax.optimization_barrier((first, weight, cotangent))
    first = exchange(first, ("x", "z"))

    arrived = [lax.ppermute(later, ("ylo", "yhi"), SPREAD[j]) for j in range(4)]
    far = trade(weight, "ylo")
    far, arrived = lax.optimization_barrier((far, arrived))
    own_core, other_core = (weight, far), (trade(weight, "core"), trade(far, "core"))
    arrived = jnp.stack(arrived)
    first, own_core, other_core, arrived = lax.optimization_barrier((first, own_core, other_core, arrived))
    summed = add_up(first[:, batch:])
    beside = trade(summed, "ylo")
    panels = first[:, :batch].reshape(2, 2, n_z, batch, block)
    panels = [
        lax.dynamic_index_in_dim(panels, c, 1, keepdims=False).transpose(0, 2, 1, 3).reshape(2 * batch, depth)
        for c in (core, 1 - core)
    ]
    frozen = [
        (dot(panels[0], own_core[i], ((1,), (0,))) + dot(panels[1], other_core[i], ((1,), (0,)))).astype(BF16)
        for i in range(2)
    ]
    frozen = jnp.stack([f.reshape(2, batch, hidden) for f in frozen], axis=1).reshape(4, batch, hidden)
    frozen = sum(
        lax.ppermute(
            lax.dynamic_index_in_dim(frozen, high ^ j ^ ylo, 0, keepdims=False), ("ylo", "yhi"), HOME[j]
        ).astype(F32)
        for j in range(4)
    )

    slabs = slabs_of(core, high ^ ylo, own_core, other_core, arrived, summed.shape[0])
    slabs, beside = lax.optimization_barrier((slabs, beside))
    summed = (summed + beside).astype(BF16)
    second = exchange(
        lax.dynamic_update_slice(slabs, to_all(summed, ("x", "z")), (0, block, 0)), ("x", "z")
    )
    kept = [lax.dynamic_index_in_dim(arrived, high ^ ylo ^ p, 0, keepdims=False) for p in (0, 2, 1, 3)]
    column = jnp.concatenate([*kept[:2], trade(jnp.concatenate(kept[2:]), "ylo")])
    second, frozen, column = lax.optimization_barrier((second, frozen, column))
    gradient = lax.ppermute(add_up(second[:, :block]), ("x", "ylo", "yhi"), BACK)
    whole = second[:, block:].reshape(share.shape)
    low, along, back_low = whole[:rank], whole[rank : rank + past], whole[rank + past :]

    projection_output = (frozen + dot(low, up, ((0,), (0,)))).astype(BF16)
    token_input_gradient = (gradient + dot(down, back_low, ((1,), (0,)))).T.astype(BF16)

    kept = tokens.astype(F32).T - dot(directions, along, ((1,), (0,)))
    kept_high = kept.astype(BF16)
    kept_rest = (kept - kept_high.astype(F32)).astype(BF16)
    down_part = dot(back_low, kept_high, ((1,), (1,))) + dot(back_low, kept_rest, ((1,), (1,)))
    pair = exchange(to_all(jnp.concatenate([low, down_part.astype(BF16)], axis=0), "yhi"), "yhi")
    lows = pair[:, :rank].reshape(2, 2, rank, batch)
    lows = [lax.dynamic_index_in_dim(lows, l, 1, keepdims=False) for l in (ylo, 1 - ylo)]
    up_part = dot(jnp.concatenate([*lows[0], *lows[1]], axis=1), column, ((1,), (0,)))
    ours = jnp.concatenate([up_part, add_up(pair[:, rank:])], axis=1)
    ours = ours + trade(ours.astype(BF16), "core").astype(F32)
    grad_up, grad_down = ours[:, :hidden], ours[:, hidden:].T
    return projection_output, token_input_gradient, grad_down, grad_up


def solution(mesh):
    fine = Mesh(mesh.devices.reshape(SIZES), AXES)
    placed = (P(DP, SHARD), P(DP, SHARD), P(SHARD, None), P(None, SHARD), P(DP, SHARD), P(SHARD, None))
    return jax.shard_map(
        local,
        mesh=fine,
        in_specs=placed,
        out_specs=(P(DP, SHARD), P(DP, SHARD), P(SHARD, None), P(None, SHARD)),
        check_vma=False,
    )
```

```python
import jax
import jax.numpy as jnp
from jax import lax
from jax.experimental import pallas as pl
from jax.experimental.pallas import tpu as pltpu
from jax.sharding import Mesh
from jax.sharding import PartitionSpec as P

F32 = jnp.float32
BF16 = jnp.bfloat16
AXES = ("x", "ylo", "z", "yhi", "core")
SIZES = (4, 2, 8, 4, 2)
SHARD = ("x", "ylo", "z")
DP = ("yhi", "core")
THERE = [
    ((x * 2 + l) * 4 + h, ((2 * (h // 2) + l) * 2 + h % 2) * 4 + x)
    for x in range(4)
    for l in range(2)
    for h in range(4)
]
BACK = [(b, a) for a, b in THERE]
HOME = [
    [(l * 4 + h, ((h ^ j) % 2) * 4 + (h ^ j) // 2 * 2 + l) for l in range(2) for h in range(4)] for j in range(4)
]


SPREAD = [
    [(l * 4 + h, (h % 2) * 4 + ((h // 2 * 2 + l) ^ j)) for l in range(2) for h in range(4)] for j in range(4)
]


def dot(left, right, contract):
    return lax.dot_general(left, right, ((contract[0], contract[1]), ((), ())), preferred_element_type=F32)


def exchange(pieces, axes):
    return lax.all_to_all(pieces, axes, split_axis=0, concat_axis=0, tiled=True)


def to_all(block, axes):
    return jnp.broadcast_to(block[None], (lax.axis_size(axes), *block.shape))


def add_up(pieces):
    return jnp.sum(pieces.astype(F32), axis=0)


def trade(block, axis):
    return lax.ppermute(block, axis, [(0, 1), (1, 0)])


def slab_kernel(where_ref, near_ref, far_ref, near_beside_ref, far_beside_ref, arrived_ref, out_ref):
    first = where_ref[1]
    block = batch = out_ref.shape[4]

    def write(own_weight, other_weight):
        total = None
        for l, weight in enumerate((own_weight, other_weight)):
            right = jnp.concatenate([arrived_ref[first ^ l], arrived_ref[first ^ l ^ 2]], axis=0)
            part = lax.dot_general(weight, right, (((1,), (1,)), ((), ())), preferred_element_type=F32)
            total = part if total is None else total + part
        total = total.astype(BF16)
        for i in range(2):
            for j in range(out_ref.shape[2]):
                out_ref[i, 0, j, :block, :] = total[j * block : (j + 1) * block, i * batch : (i + 1) * batch]

    @pl.when(pl.program_id(0) == 0)
    def _():
        write(near_ref[...], far_ref[...])

    @pl.when(pl.program_id(0) == 1)
    def _():
        write(near_beside_ref[...], far_beside_ref[...])


def slabs_of(core, first, own_core, other_core, arrived, extra):
    batch = arrived.shape[1]
    block, take = batch, 4
    depth, hidden = own_core[0].shape
    steps = depth // (take * block)
    early = pl.BlockSpec((take * block, hidden), lambda s, r, _: (jnp.where(s == 0, r, steps - 1), 0))
    late = pl.BlockSpec((take * block, hidden), lambda s, r, _: (jnp.where(s == 0, 0, r), 0))
    whole = pl.BlockSpec(arrived.shape, lambda s, r, _: (0, 0, 0))
    out = pl.pallas_call(
        slab_kernel,
        grid_spec=pltpu.PrefetchScalarGridSpec(
            num_scalar_prefetch=1,
            grid=(2, steps),
            in_specs=[early, early, late, late, whole],
            out_specs=pl.BlockSpec(
                (2, 1, take, block + extra, batch), lambda s, r, c: (0, s ^ c[0], r, 0, 0)
            ),
        ),
        out_shape=jax.ShapeDtypeStruct((2, 2, steps * take, block + extra, batch), BF16),
        cost_estimate=pl.CostEstimate(
            flops=16 * depth * hidden * batch, bytes_accessed=8 * depth * hidden, transcendentals=0
        ),
    )(jnp.stack([core, first]), *own_core, *other_core, arrived)
    return out.reshape(4 * steps * take, block + extra, batch)


def local(tokens, weight, down, up, cotangent, directions):
    n_z = lax.axis_size("z")
    batch, block = tokens.shape
    rank = down.shape[1]
    past = directions.shape[1]
    depth, hidden = weight.shape

    ylo, high, core = (lax.axis_index(a) for a in ("ylo", "yhi", "core"))
    moved = lax.ppermute(tokens, ("x", "ylo", "yhi"), THERE)

    share = jnp.concatenate(
        [
            dot(down, tokens, ((0,), (1,))),
            dot(directions, tokens, ((0,), (1,))),
            dot(up, cotangent, ((1,), (1,))),
        ],
        axis=0,
    ).astype(BF16)
    first = jnp.concatenate([to_all(moved, ("x", "z")), share.reshape(4 * n_z, -1, batch)], axis=1)
    first, weight, later = lax.optimization_barrier((first, weight, cotangent))
    first = exchange(first, ("x", "z"))

    arrived = [lax.ppermute(later, ("ylo", "yhi"), SPREAD[j]) for j in range(4)]
    far = trade(weight, "ylo")
    far, arrived = lax.optimization_barrier((far, arrived))
    own_core, other_core = (weight, far), (trade(weight, "core"), trade(far, "core"))
    arrived = jnp.stack(arrived)
    first, own_core, other_core, arrived = lax.optimization_barrier((first, own_core, other_core, arrived))
    summed = add_up(first[:, batch:])
    beside = trade(summed, "ylo")
    panels = first[:, :batch].reshape(2, 2, n_z, batch, block)
    panels = [
        lax.dynamic_index_in_dim(panels, c, 1, keepdims=False).transpose(0, 2, 1, 3).reshape(2 * batch, depth)
        for c in (core, 1 - core)
    ]
    frozen = [
        (dot(panels[0], own_core[i], ((1,), (0,))) + dot(panels[1], other_core[i], ((1,), (0,)))).astype(BF16)
        for i in range(2)
    ]
    frozen = jnp.stack([f.reshape(2, batch, hidden) for f in frozen], axis=1).reshape(4, batch, hidden)
    kept = [lax.dynamic_index_in_dim(arrived, high ^ ylo ^ p, 0, keepdims=False) for p in (0, 2, 1, 3)]
    column = jnp.concatenate([*kept[:2], trade(jnp.concatenate(kept[2:]), "ylo")])
    frozen, column = lax.optimization_barrier((frozen, column))
    frozen = sum(
        lax.ppermute(
            lax.dynamic_index_in_dim(frozen, high ^ j ^ ylo, 0, keepdims=False), ("ylo", "yhi"), HOME[j]
        ).astype(F32)
        for j in range(4)
    )

    slabs = slabs_of(core, high ^ ylo, own_core, other_core, arrived, summed.shape[0])
    slabs, beside = lax.optimization_barrier((slabs, beside))
    summed = (summed + beside).astype(BF16)
    second = exchange(
        lax.dynamic_update_slice(slabs, to_all(summed, ("x", "z")), (0, block, 0)), ("x", "z")
    )
    second, frozen = lax.optimization_barrier((second, frozen))
    gradient = lax.ppermute(add_up(second[:, :block]), ("x", "ylo", "yhi"), BACK)
    whole = second[:, block:].reshape(share.shape)
    low, along, back_low = whole[:rank], whole[rank : rank + past], whole[rank + past :]

    projection_output = (frozen + dot(low, up, ((0,), (0,)))).astype(BF16)
    token_input_gradient = (gradient + dot(down, back_low, ((1,), (0,)))).T.astype(BF16)

    kept = tokens.astype(F32).T - dot(directions, along, ((1,), (0,)))
    kept_high = kept.astype(BF16)
    kept_rest = (kept - kept_high.astype(F32)).astype(BF16)
    down_part = dot(back_low, kept_high, ((1,), (1,))) + dot(back_low, kept_rest, ((1,), (1,)))
    pair = exchange(to_all(jnp.concatenate([low, down_part.astype(BF16)], axis=0), "yhi"), "yhi")
    lows = pair[:, :rank].reshape(2, 2, rank, batch)
    lows = [lax.dynamic_index_in_dim(lows, l, 1, keepdims=False) for l in (ylo, 1 - ylo)]
    up_part = dot(jnp.concatenate([*lows[0], *lows[1]], axis=1), column, ((1,), (0,)))
    ours = jnp.concatenate([up_part, add_up(pair[:, rank:])], axis=1)
    ours = ours + trade(ours.astype(BF16), "core").astype(F32)
    grad_up, grad_down = ours[:, :hidden], ours[:, hidden:].T
    return projection_output, token_input_gradient, grad_down, grad_up


def solution(mesh):
    fine = Mesh(mesh.devices.reshape(SIZES), AXES)
    placed = (P(DP, SHARD), P(DP, SHARD), P(SHARD, None), P(None, SHARD), P(DP, SHARD), P(SHARD, None))
    return jax.shard_map(
        local,
        mesh=fine,
        in_specs=placed,
        out_specs=(P(DP, SHARD), P(DP, SHARD), P(SHARD, None), P(None, SHARD)),
        check_vma=False,
    )
```

```python
import jax
import jax.numpy as jnp
from jax import lax
from jax.experimental import pallas as pl
from jax.experimental.pallas import tpu as pltpu
from jax.sharding import Mesh
from jax.sharding import PartitionSpec as P

F32 = jnp.float32
BF16 = jnp.bfloat16
AXES = ("x", "ylo", "z", "yhi", "core")
SIZES = (4, 2, 8, 4, 2)
SHARD = ("x", "ylo", "z")
DP = ("yhi", "core")
THERE = [
    ((x * 2 + l) * 4 + h, ((2 * (h // 2) + l) * 2 + h % 2) * 4 + x)
    for x in range(4)
    for l in range(2)
    for h in range(4)
]
BACK = [(b, a) for a, b in THERE]
HOME = [
    [(l * 4 + h, ((h ^ j) % 2) * 4 + (h ^ j) // 2 * 2 + l) for l in range(2) for h in range(4)] for j in range(4)
]


SPREAD = [
    [(l * 4 + h, (h % 2) * 4 + ((h // 2 * 2 + l) ^ j)) for l in range(2) for h in range(4)] for j in range(4)
]


def dot(left, right, contract):
    return lax.dot_general(left, right, ((contract[0], contract[1]), ((), ())), preferred_element_type=F32)


def exchange(pieces, axes):
    return lax.all_to_all(pieces, axes, split_axis=0, concat_axis=0, tiled=True)


def to_all(block, axes):
    return jnp.broadcast_to(block[None], (lax.axis_size(axes), *block.shape))


def add_up(pieces):
    return jnp.sum(pieces.astype(F32), axis=0)


def trade(block, axis):
    return lax.ppermute(block, axis, [(0, 1), (1, 0)])


def slab_kernel(where_ref, near_ref, far_ref, near_beside_ref, far_beside_ref, arrived_ref, out_ref):
    first = where_ref[1]
    block = batch = out_ref.shape[4]

    def write(own_weight, other_weight):
        total = None
        for l, weight in enumerate((own_weight, other_weight)):
            right = jnp.concatenate([arrived_ref[first ^ l], arrived_ref[first ^ l ^ 2]], axis=0)
            part = lax.dot_general(weight, right, (((1,), (1,)), ((), ())), preferred_element_type=F32)
            total = part if total is None else total + part
        total = total.astype(BF16)
        for i in range(2):
            for j in range(out_ref.shape[2]):
                out_ref[i, 0, j, :block, :] = total[j * block : (j + 1) * block, i * batch : (i + 1) * batch]

    @pl.when(pl.program_id(0) == 0)
    def _():
        write(near_ref[...], far_ref[...])

    @pl.when(pl.program_id(0) == 1)
    def _():
        write(near_beside_ref[...], far_beside_ref[...])


def slabs_of(core, first, own_core, other_core, arrived, extra):
    batch = arrived.shape[1]
    block, take = batch, 4
    depth, hidden = own_core[0].shape
    steps = depth // (take * block)
    early = pl.BlockSpec((take * block, hidden), lambda s, r, _: (jnp.where(s == 0, r, steps - 1), 0))
    late = pl.BlockSpec((take * block, hidden), lambda s, r, _: (jnp.where(s == 0, 0, r), 0))
    whole = pl.BlockSpec(arrived.shape, lambda s, r, _: (0, 0, 0))
    out = pl.pallas_call(
        slab_kernel,
        grid_spec=pltpu.PrefetchScalarGridSpec(
            num_scalar_prefetch=1,
            grid=(2, steps),
            in_specs=[early, early, late, late, whole],
            out_specs=pl.BlockSpec(
                (2, 1, take, block + extra, batch), lambda s, r, c: (0, s ^ c[0], r, 0, 0)
            ),
        ),
        out_shape=jax.ShapeDtypeStruct((2, 2, steps * take, block + extra, batch), BF16),
        cost_estimate=pl.CostEstimate(
            flops=16 * depth * hidden * batch, bytes_accessed=8 * depth * hidden, transcendentals=0
        ),
    )(jnp.stack([core, first]), *own_core, *other_core, arrived)
    return out.reshape(4 * steps * take, block + extra, batch)


def local(tokens, weight, down, up, cotangent, directions):
    n_z = lax.axis_size("z")
    batch, block = tokens.shape
    rank = down.shape[1]
    past = directions.shape[1]
    depth, hidden = weight.shape

    ylo, high, core = (lax.axis_index(a) for a in ("ylo", "yhi", "core"))
    moved = lax.ppermute(tokens, ("x", "ylo", "yhi"), THERE)
    moved, weight = lax.optimization_barrier((moved, weight))
    far = trade(weight, "ylo")

    share = jnp.concatenate(
        [
            dot(down, tokens, ((0,), (1,))),
            dot(directions, tokens, ((0,), (1,))),
            dot(up, cotangent, ((1,), (1,))),
        ],
        axis=0,
    ).astype(BF16)
    first = jnp.concatenate([to_all(moved, ("x", "z")), share.reshape(4 * n_z, -1, batch)], axis=1)
    first, weight, later = lax.optimization_barrier((first, weight, cotangent))
    first = exchange(first, ("x", "z"))

    arrived = [lax.ppermute(later, ("ylo", "yhi"), SPREAD[j]) for j in range(4)]
    far, arrived = lax.optimization_barrier((far, arrived))
    own_core, other_core = (weight, far), (trade(weight, "core"), trade(far, "core"))
    arrived = jnp.stack(arrived)
    first, own_core, other_core, arrived = lax.optimization_barrier((first, own_core, other_core, arrived))
    summed = add_up(first[:, batch:])
    beside = trade(summed, "ylo")
    panels = first[:, :batch].reshape(2, 2, n_z, batch, block)
    panels = [
        lax.dynamic_index_in_dim(panels, c, 1, keepdims=False).transpose(0, 2, 1, 3).reshape(2 * batch, depth)
        for c in (core, 1 - core)
    ]
    frozen = [
        (dot(panels[0], own_core[i], ((1,), (0,))) + dot(panels[1], other_core[i], ((1,), (0,)))).astype(BF16)
        for i in range(2)
    ]
    frozen = jnp.stack([f.reshape(2, batch, hidden) for f in frozen], axis=1).reshape(4, batch, hidden)
    kept = [lax.dynamic_index_in_dim(arrived, high ^ ylo ^ p, 0, keepdims=False) for p in (0, 2, 1, 3)]
    column = jnp.concatenate([*kept[:2], trade(jnp.concatenate(kept[2:]), "ylo")])
    frozen, column = lax.optimization_barrier((frozen, column))
    frozen = sum(
        lax.ppermute(
            lax.dynamic_index_in_dim(frozen, high ^ j ^ ylo, 0, keepdims=False), ("ylo", "yhi"), HOME[j]
        ).astype(F32)
        for j in range(4)
    )

    slabs = slabs_of(core, high ^ ylo, own_core, other_core, arrived, summed.shape[0])
    slabs, beside = lax.optimization_barrier((slabs, beside))
    summed = (summed + beside).astype(BF16)
    second = exchange(
        lax.dynamic_update_slice(slabs, to_all(summed, ("x", "z")), (0, block, 0)), ("x", "z")
    )
    second, frozen = lax.optimization_barrier((second, frozen))
    gradient = lax.ppermute(add_up(second[:, :block]), ("x", "ylo", "yhi"), BACK)
    whole = second[:, block:].reshape(share.shape)
    low, along, back_low = whole[:rank], whole[rank : rank + past], whole[rank + past :]

    projection_output = (frozen + dot(low, up, ((0,), (0,)))).astype(BF16)
    token_input_gradient = (gradient + dot(down, back_low, ((1,), (0,)))).T.astype(BF16)

    kept = tokens.astype(F32).T - dot(directions, along, ((1,), (0,)))
    kept_high = kept.astype(BF16)
    kept_rest = (kept - kept_high.astype(F32)).astype(BF16)
    down_part = dot(back_low, kept_high, ((1,), (1,))) + dot(back_low, kept_rest, ((1,), (1,)))
    pair = exchange(to_all(jnp.concatenate([low, down_part.astype(BF16)], axis=0), "yhi"), "yhi")
    lows = pair[:, :rank].reshape(2, 2, rank, batch)
    lows = [lax.dynamic_index_in_dim(lows, l, 1, keepdims=False) for l in (ylo, 1 - ylo)]
    up_part = dot(jnp.concatenate([*lows[0], *lows[1]], axis=1), column, ((1,), (0,)))
    ours = jnp.concatenate([up_part, add_up(pair[:, rank:])], axis=1)
    ours = ours + trade(ours.astype(BF16), "core").astype(F32)
    grad_up, grad_down = ours[:, :hidden], ours[:, hidden:].T
    return projection_output, token_input_gradient, grad_down, grad_up


def solution(mesh):
    fine = Mesh(mesh.devices.reshape(SIZES), AXES)
    placed = (P(DP, SHARD), P(DP, SHARD), P(SHARD, None), P(None, SHARD), P(DP, SHARD), P(SHARD, None))
    return jax.shard_map(
        local,
        mesh=fine,
        in_specs=placed,
        out_specs=(P(DP, SHARD), P(DP, SHARD), P(SHARD, None), P(None, SHARD)),
        check_vma=False,
    )
```

```python
import jax
import jax.numpy as jnp
from jax import lax
from jax.experimental import pallas as pl
from jax.experimental.pallas import tpu as pltpu
from jax.sharding import Mesh
from jax.sharding import PartitionSpec as P

F32 = jnp.float32
BF16 = jnp.bfloat16
AXES = ("x", "ylo", "z", "yhi", "core")
SIZES = (4, 2, 8, 4, 2)
SHARD = ("x", "ylo", "z")
DP = ("yhi", "core")
THERE = [
    ((x * 2 + l) * 4 + h, ((2 * (h // 2) + l) * 2 + h % 2) * 4 + x)
    for x in range(4)
    for l in range(2)
    for h in range(4)
]
BACK = [(b, a) for a, b in THERE]
HOME = [
    [(l * 4 + h, ((h ^ j) % 2) * 4 + (h ^ j) // 2 * 2 + l) for l in range(2) for h in range(4)] for j in range(4)
]


SPREAD = [
    [(l * 4 + h, (h % 2) * 4 + ((h // 2 * 2 + l) ^ j)) for l in range(2) for h in range(4)] for j in range(4)
]


def dot(left, right, contract):
    return lax.dot_general(left, right, ((contract[0], contract[1]), ((), ())), preferred_element_type=F32)


def exchange(pieces, axes):
    return lax.all_to_all(pieces, axes, split_axis=0, concat_axis=0, tiled=True)


def to_all(block, axes):
    return jnp.broadcast_to(block[None], (lax.axis_size(axes), *block.shape))


def add_up(pieces):
    return jnp.sum(pieces.astype(F32), axis=0)


def trade(block, axis):
    return lax.ppermute(block, axis, [(0, 1), (1, 0)])


def slab_kernel(where_ref, near_ref, far_ref, near_beside_ref, far_beside_ref, arrived_ref, out_ref):
    first = where_ref[1]
    block = batch = out_ref.shape[4]

    def write(own_weight, other_weight):
        total = None
        for l, weight in enumerate((own_weight, other_weight)):
            right = jnp.concatenate([arrived_ref[first ^ l], arrived_ref[first ^ l ^ 2]], axis=0)
            part = lax.dot_general(weight, right, (((1,), (1,)), ((), ())), preferred_element_type=F32)
            total = part if total is None else total + part
        total = total.astype(BF16)
        for i in range(2):
            for j in range(out_ref.shape[2]):
                out_ref[i, 0, j, :block, :] = total[j * block : (j + 1) * block, i * batch : (i + 1) * batch]

    @pl.when(pl.program_id(0) == 0)
    def _():
        write(near_ref[...], far_ref[...])

    @pl.when(pl.program_id(0) == 1)
    def _():
        write(near_beside_ref[...], far_beside_ref[...])


def slabs_of(core, first, own_core, other_core, arrived, extra):
    batch = arrived.shape[1]
    block, take = batch, 4
    depth, hidden = own_core[0].shape
    steps = depth // (take * block)
    early = pl.BlockSpec((take * block, hidden), lambda s, r, _: (jnp.where(s == 0, r, steps - 1), 0))
    late = pl.BlockSpec((take * block, hidden), lambda s, r, _: (jnp.where(s == 0, 0, r), 0))
    whole = pl.BlockSpec(arrived.shape, lambda s, r, _: (0, 0, 0))
    out = pl.pallas_call(
        slab_kernel,
        grid_spec=pltpu.PrefetchScalarGridSpec(
            num_scalar_prefetch=1,
            grid=(2, steps),
            in_specs=[early, early, late, late, whole],
            out_specs=pl.BlockSpec(
                (2, 1, take, block + extra, batch), lambda s, r, c: (0, s ^ c[0], r, 0, 0)
            ),
        ),
        out_shape=jax.ShapeDtypeStruct((2, 2, steps * take, block + extra, batch), BF16),
        cost_estimate=pl.CostEstimate(
            flops=16 * depth * hidden * batch, bytes_accessed=8 * depth * hidden, transcendentals=0
        ),
    )(jnp.stack([core, first]), *own_core, *other_core, arrived)
    return out.reshape(4 * steps * take, block + extra, batch)


def local(tokens, weight, down, up, cotangent, directions):
    n_z = lax.axis_size("z")
    batch, block = tokens.shape
    rank = down.shape[1]
    past = directions.shape[1]
    depth, hidden = weight.shape

    ylo, high, core = (lax.axis_index(a) for a in ("ylo", "yhi", "core"))
    moved = lax.ppermute(tokens, ("x", "ylo", "yhi"), THERE)
    moved, weight = lax.optimization_barrier((moved, weight))
    far = trade(weight, "ylo")

    share = jnp.concatenate(
        [
            dot(down, tokens, ((0,), (1,))),
            dot(directions, tokens, ((0,), (1,))),
            dot(up, cotangent, ((1,), (1,))),
        ],
        axis=0,
    ).astype(BF16)
    first = jnp.concatenate([to_all(moved, ("x", "z")), share.reshape(4 * n_z, -1, batch)], axis=1)
    first, weight, later = lax.optimization_barrier((first, weight, cotangent))
    first = exchange(first, ("x", "z"))

    arrived = [lax.ppermute(later, ("ylo", "yhi"), SPREAD[j]) for j in range(4)]
    far, arrived = lax.optimization_barrier((far, arrived))
    own_core, other_core = (weight, far), (trade(weight, "core"), trade(far, "core"))
    arrived = jnp.stack(arrived)
    first, own_core, other_core, arrived = lax.optimization_barrier((first, own_core, other_core, arrived))
    summed = add_up(first[:, batch:])
    beside = trade(summed, "ylo")
    panels = first[:, :batch].reshape(2, 2, n_z, batch, block)
    panels = [
        lax.dynamic_index_in_dim(panels, c, 1, keepdims=False).transpose(0, 2, 1, 3).reshape(2 * batch, depth)
        for c in (core, 1 - core)
    ]
    frozen = [
        (dot(panels[0], own_core[i], ((1,), (0,))) + dot(panels[1], other_core[i], ((1,), (0,)))).astype(BF16)
        for i in range(2)
    ]
    frozen = jnp.stack([f.reshape(2, batch, hidden) for f in frozen], axis=1).reshape(4, batch, hidden)
    kept = [lax.dynamic_index_in_dim(arrived, high ^ ylo ^ p, 0, keepdims=False) for p in (0, 2, 1, 3)]
    column = jnp.concatenate([*kept[:2], trade(jnp.concatenate(kept[2:]), "ylo")])
    column = column.reshape(4, batch, hidden)
    order = [2 * ((high ^ j ^ ylo) & 1) + ((high ^ j) >> 1) for j in range(4)]
    column = jnp.concatenate([lax.dynamic_index_in_dim(column, i, 0, keepdims=False) for i in order])
    frozen, column = lax.optimization_barrier((frozen, column))
    frozen = sum(
        lax.ppermute(
            lax.dynamic_index_in_dim(frozen, high ^ j ^ ylo, 0, keepdims=False), ("ylo", "yhi"), HOME[j]
        ).astype(F32)
        for j in range(4)
    )

    slabs = slabs_of(core, high ^ ylo, own_core, other_core, arrived, summed.shape[0])
    slabs, beside = lax.optimization_barrier((slabs, beside))
    summed = (summed + beside).astype(BF16)
    second = exchange(
        lax.dynamic_update_slice(slabs, to_all(summed, ("x", "z")), (0, block, 0)), ("x", "z")
    )
    second, frozen = lax.optimization_barrier((second, frozen))
    gradient = lax.ppermute(add_up(second[:, :block]), ("x", "ylo", "yhi"), BACK)
    whole = second[:, block:].reshape(share.shape)
    low, along, back_low = whole[:rank], whole[rank : rank + past], whole[rank + past :]

    projection_output = (frozen + dot(low, up, ((0,), (0,)))).astype(BF16)
    token_input_gradient = (gradient + dot(down, back_low, ((1,), (0,)))).T.astype(BF16)

    kept = tokens.astype(F32).T - dot(directions, along, ((1,), (0,)))
    kept_high = kept.astype(BF16)
    kept_rest = (kept - kept_high.astype(F32)).astype(BF16)
    down_part = dot(back_low, kept_high, ((1,), (1,))) + dot(back_low, kept_rest, ((1,), (1,)))
    pair = jnp.concatenate([low, down_part.astype(BF16)], axis=0)
    pair = [pair] + [lax.ppermute(pair, "yhi", [(h, h ^ j) for h in range(4)]) for j in range(1, 4)]
    up_part = dot(jnp.concatenate([p[:rank] for p in pair], axis=1), column, ((1,), (0,)))
    down_part = sum(p[rank:].astype(F32) for p in pair)
    ours = jnp.concatenate([up_part, down_part], axis=1)
    ours = ours + trade(ours.astype(BF16), "core").astype(F32)
    grad_up, grad_down = ours[:, :hidden], ours[:, hidden:].T
    return projection_output, token_input_gradient, grad_down, grad_up


def solution(mesh):
    fine = Mesh(mesh.devices.reshape(SIZES), AXES)
    placed = (P(DP, SHARD), P(DP, SHARD), P(SHARD, None), P(None, SHARD), P(DP, SHARD), P(SHARD, None))
    return jax.shard_map(
        local,
        mesh=fine,
        in_specs=placed,
        out_specs=(P(DP, SHARD), P(DP, SHARD), P(SHARD, None), P(None, SHARD)),
        check_vma=False,
    )
```

```python
import jax
import jax.numpy as jnp
from jax import lax
from jax.experimental import pallas as pl
from jax.experimental.pallas import tpu as pltpu
from jax.sharding import Mesh
from jax.sharding import PartitionSpec as P

F32 = jnp.float32
BF16 = jnp.bfloat16
AXES = ("x", "ylo", "z", "yhi", "core")
SIZES = (4, 2, 8, 4, 2)
SHARD = ("x", "ylo", "z")
DP = ("yhi", "core")
THERE = [
    ((x * 2 + l) * 4 + h, ((2 * (h // 2) + l) * 2 + h % 2) * 4 + x)
    for x in range(4)
    for l in range(2)
    for h in range(4)
]
BACK = [(b, a) for a, b in THERE]
HOME = [
    [(l * 4 + h, ((h ^ j) % 2) * 4 + (h ^ j) // 2 * 2 + l) for l in range(2) for h in range(4)] for j in range(4)
]


SPREAD = [
    [(l * 4 + h, (h % 2) * 4 + ((h // 2 * 2 + l) ^ j)) for l in range(2) for h in range(4)] for j in range(4)
]


def dot(left, right, contract):
    return lax.dot_general(left, right, ((contract[0], contract[1]), ((), ())), preferred_element_type=F32)


def exchange(pieces, axes):
    return lax.all_to_all(pieces, axes, split_axis=0, concat_axis=0, tiled=True)


def to_all(block, axes):
    return jnp.broadcast_to(block[None], (lax.axis_size(axes), *block.shape))


def add_up(pieces):
    return jnp.sum(pieces.astype(F32), axis=0)


def trade(block, axis):
    return lax.ppermute(block, axis, [(0, 1), (1, 0)])


def slab_kernel(where_ref, near_ref, far_ref, near_beside_ref, far_beside_ref, arrived_ref, out_ref):
    first = where_ref[1]
    block = batch = out_ref.shape[4]

    def write(own_weight, other_weight):
        total = None
        for l, weight in enumerate((own_weight, other_weight)):
            right = jnp.concatenate([arrived_ref[first ^ l], arrived_ref[first ^ l ^ 2]], axis=0)
            part = lax.dot_general(weight, right, (((1,), (1,)), ((), ())), preferred_element_type=F32)
            total = part if total is None else total + part
        total = total.astype(BF16)
        for i in range(2):
            for j in range(out_ref.shape[2]):
                out_ref[i, 0, j, :block, :] = total[j * block : (j + 1) * block, i * batch : (i + 1) * batch]

    @pl.when(pl.program_id(0) == 0)
    def _():
        write(near_ref[...], far_ref[...])

    @pl.when(pl.program_id(0) == 1)
    def _():
        write(near_beside_ref[...], far_beside_ref[...])


def slabs_of(core, first, own_core, other_core, arrived, extra):
    batch = arrived.shape[1]
    block, take = batch, 4
    depth, hidden = own_core[0].shape
    steps = depth // (take * block)
    early = pl.BlockSpec((take * block, hidden), lambda s, r, _: (jnp.where(s == 0, r, steps - 1), 0))
    late = pl.BlockSpec((take * block, hidden), lambda s, r, _: (jnp.where(s == 0, 0, r), 0))
    whole = pl.BlockSpec(arrived.shape, lambda s, r, _: (0, 0, 0))
    out = pl.pallas_call(
        slab_kernel,
        grid_spec=pltpu.PrefetchScalarGridSpec(
            num_scalar_prefetch=1,
            grid=(2, steps),
            in_specs=[early, early, late, late, whole],
            out_specs=pl.BlockSpec(
                (2, 1, take, block + extra, batch), lambda s, r, c: (0, s ^ c[0], r, 0, 0)
            ),
        ),
        out_shape=jax.ShapeDtypeStruct((2, 2, steps * take, block + extra, batch), BF16),
        cost_estimate=pl.CostEstimate(
            flops=16 * depth * hidden * batch, bytes_accessed=8 * depth * hidden, transcendentals=0
        ),
    )(jnp.stack([core, first]), *own_core, *other_core, arrived)
    return out.reshape(4 * steps * take, block + extra, batch)


def local(tokens, weight, down, up, cotangent, directions):
    n_z = lax.axis_size("z")
    batch, block = tokens.shape
    rank = down.shape[1]
    past = directions.shape[1]
    depth, hidden = weight.shape

    ylo, high, core = (lax.axis_index(a) for a in ("ylo", "yhi", "core"))
    moved = lax.ppermute(tokens, ("x", "ylo", "yhi"), THERE)
    moved, weight = lax.optimization_barrier((moved, weight))
    far = trade(weight, "ylo")

    share = jnp.concatenate(
        [
            dot(down, tokens, ((0,), (1,))),
            dot(directions, tokens, ((0,), (1,))),
            dot(up, cotangent, ((1,), (1,))),
        ],
        axis=0,
    ).astype(BF16)
    first = jnp.concatenate([to_all(moved, ("x", "z")), share.reshape(4 * n_z, -1, batch)], axis=1)
    first, weight, later = lax.optimization_barrier((first, weight, cotangent))
    first = exchange(first, ("x", "z"))

    arrived = [lax.ppermute(later, ("ylo", "yhi"), SPREAD[j]) for j in range(4)]
    far, arrived[0], arrived[1], arrived[3] = lax.optimization_barrier((far, arrived[0], arrived[1], arrived[3]))
    own_core, other_core = (weight, far), (trade(weight, "core"), trade(far, "core"))
    arrived = jnp.stack(arrived)
    first, own_core, other_core, arrived = lax.optimization_barrier((first, own_core, other_core, arrived))
    summed = add_up(first[:, batch:])
    beside = trade(summed, "ylo")
    panels = first[:, :batch].reshape(2, 2, n_z, batch, block)
    panels = [
        lax.dynamic_index_in_dim(panels, c, 1, keepdims=False).transpose(0, 2, 1, 3).reshape(2 * batch, depth)
        for c in (core, 1 - core)
    ]
    frozen = [
        (dot(panels[0], own_core[i], ((1,), (0,))) + dot(panels[1], other_core[i], ((1,), (0,)))).astype(BF16)
        for i in range(2)
    ]
    frozen = jnp.stack([f.reshape(2, batch, hidden) for f in frozen], axis=1).reshape(4, batch, hidden)
    kept = [lax.dynamic_index_in_dim(arrived, high ^ ylo ^ p, 0, keepdims=False) for p in (0, 2, 1, 3)]
    column = jnp.concatenate([*kept[:2], trade(jnp.concatenate(kept[2:]), "ylo")])
    frozen, column = lax.optimization_barrier((frozen, column))
    frozen = sum(
        lax.ppermute(
            lax.dynamic_index_in_dim(frozen, high ^ j ^ ylo, 0, keepdims=False), ("ylo", "yhi"), HOME[j]
        ).astype(F32)
        for j in range(4)
    )

    slabs = slabs_of(core, high ^ ylo, own_core, other_core, arrived, summed.shape[0])
    slabs, beside = lax.optimization_barrier((slabs, beside))
    summed = (summed + beside).astype(BF16)
    second = exchange(
        lax.dynamic_update_slice(slabs, to_all(summed, ("x", "z")), (0, block, 0)), ("x", "z")
    )
    second, frozen = lax.optimization_barrier((second, frozen))
    gradient = lax.ppermute(add_up(second[:, :block]), ("x", "ylo", "yhi"), BACK)
    whole = second[:, block:].reshape(share.shape)
    low, along, back_low = whole[:rank], whole[rank : rank + past], whole[rank + past :]

    projection_output = (frozen + dot(low, up, ((0,), (0,)))).astype(BF16)
    token_input_gradient = (gradient + dot(down, back_low, ((1,), (0,)))).T.astype(BF16)

    kept = tokens.astype(F32).T - dot(directions, along, ((1,), (0,)))
    kept_high = kept.astype(BF16)
    kept_rest = (kept - kept_high.astype(F32)).astype(BF16)
    down_part = dot(back_low, kept_high, ((1,), (1,))) + dot(back_low, kept_rest, ((1,), (1,)))
    pair = exchange(to_all(jnp.concatenate([low, down_part.astype(BF16)], axis=0), "yhi"), "yhi")
    lows = pair[:, :rank].reshape(2, 2, rank, batch)
    lows = [lax.dynamic_index_in_dim(lows, l, 1, keepdims=False) for l in (ylo, 1 - ylo)]
    up_part = dot(jnp.concatenate([*lows[0], *lows[1]], axis=1), column, ((1,), (0,)))
    ours = jnp.concatenate([up_part, add_up(pair[:, rank:])], axis=1)
    ours = ours + trade(ours.astype(BF16), "core").astype(F32)
    grad_up, grad_down = ours[:, :hidden], ours[:, hidden:].T
    return projection_output, token_input_gradient, grad_down, grad_up


def solution(mesh):
    fine = Mesh(mesh.devices.reshape(SIZES), AXES)
    placed = (P(DP, SHARD), P(DP, SHARD), P(SHARD, None), P(None, SHARD), P(DP, SHARD), P(SHARD, None))
    return jax.shard_map(
        local,
        mesh=fine,
        in_specs=placed,
        out_specs=(P(DP, SHARD), P(DP, SHARD), P(SHARD, None), P(None, SHARD)),
        check_vma=False,
    )
```

```python
import jax
import jax.numpy as jnp
from jax import lax
from jax.experimental import pallas as pl
from jax.experimental.pallas import tpu as pltpu
from jax.sharding import Mesh
from jax.sharding import PartitionSpec as P

F32 = jnp.float32
BF16 = jnp.bfloat16
AXES = ("x", "ylo", "z", "yhi", "core")
SIZES = (4, 2, 8, 4, 2)
SHARD = ("x", "ylo", "z")
DP = ("yhi", "core")
THERE = [
    ((x * 2 + l) * 4 + h, ((2 * (h // 2) + l) * 2 + h % 2) * 4 + x)
    for x in range(4)
    for l in range(2)
    for h in range(4)
]
BACK = [(b, a) for a, b in THERE]
HOME = [
    [(l * 4 + h, ((h ^ j) % 2) * 4 + (h ^ j) // 2 * 2 + l) for l in range(2) for h in range(4)] for j in range(4)
]


SPREAD = [
    [(l * 4 + h, (h % 2) * 4 + ((h // 2 * 2 + l) ^ j)) for l in range(2) for h in range(4)] for j in range(4)
]


def dot(left, right, contract):
    return lax.dot_general(left, right, ((contract[0], contract[1]), ((), ())), preferred_element_type=F32)


def exchange(pieces, axes):
    return lax.all_to_all(pieces, axes, split_axis=0, concat_axis=0, tiled=True)


def to_all(block, axes):
    return jnp.broadcast_to(block[None], (lax.axis_size(axes), *block.shape))


def add_up(pieces):
    return jnp.sum(pieces.astype(F32), axis=0)


def trade(block, axis):
    return lax.ppermute(block, axis, [(0, 1), (1, 0)])


def slab_kernel(where_ref, near_ref, far_ref, near_beside_ref, far_beside_ref, arrived_ref, out_ref):
    first = where_ref[1]
    block = batch = out_ref.shape[4]

    def write(own_weight, other_weight):
        total = None
        for l, weight in enumerate((own_weight, other_weight)):
            right = jnp.concatenate([arrived_ref[first ^ l], arrived_ref[first ^ l ^ 2]], axis=0)
            part = lax.dot_general(weight, right, (((1,), (1,)), ((), ())), preferred_element_type=F32)
            total = part if total is None else total + part
        total = total.astype(BF16)
        for i in range(2):
            for j in range(out_ref.shape[2]):
                out_ref[i, 0, j, :block, :] = total[j * block : (j + 1) * block, i * batch : (i + 1) * batch]

    @pl.when(pl.program_id(0) == 0)
    def _():
        write(near_ref[...], far_ref[...])

    @pl.when(pl.program_id(0) == 1)
    def _():
        write(near_beside_ref[...], far_beside_ref[...])


def slabs_of(core, first, own_core, other_core, arrived, extra):
    batch = arrived.shape[1]
    block, take = batch, 4
    depth, hidden = own_core[0].shape
    steps = depth // (take * block)
    early = pl.BlockSpec((take * block, hidden), lambda s, r, _: (jnp.where(s == 0, r, steps - 1), 0))
    late = pl.BlockSpec((take * block, hidden), lambda s, r, _: (jnp.where(s == 0, 0, r), 0))
    whole = pl.BlockSpec(arrived.shape, lambda s, r, _: (0, 0, 0))
    out = pl.pallas_call(
        slab_kernel,
        grid_spec=pltpu.PrefetchScalarGridSpec(
            num_scalar_prefetch=1,
            grid=(2, steps),
            in_specs=[early, early, late, late, whole],
            out_specs=pl.BlockSpec(
                (2, 1, take, block + extra, batch), lambda s, r, c: (0, s ^ c[0], r, 0, 0)
            ),
        ),
        out_shape=jax.ShapeDtypeStruct((2, 2, steps * take, block + extra, batch), BF16),
        cost_estimate=pl.CostEstimate(
            flops=16 * depth * hidden * batch, bytes_accessed=8 * depth * hidden, transcendentals=0
        ),
    )(jnp.stack([core, first]), *own_core, *other_core, arrived)
    return out.reshape(4 * steps * take, block + extra, batch)


def local(tokens, weight, down, up, cotangent, directions):
    n_z = lax.axis_size("z")
    batch, block = tokens.shape
    rank = down.shape[1]
    past = directions.shape[1]
    depth, hidden = weight.shape

    ylo, high, core = (lax.axis_index(a) for a in ("ylo", "yhi", "core"))
    moved = lax.ppermute(tokens, ("x", "ylo", "yhi"), THERE)
    moved, weight = lax.optimization_barrier((moved, weight))
    far = trade(weight, "ylo")

    share = jnp.concatenate(
        [
            dot(down, tokens, ((0,), (1,))),
            dot(directions, tokens, ((0,), (1,))),
            dot(up, cotangent, ((1,), (1,))),
        ],
        axis=0,
    ).astype(BF16)
    first = jnp.concatenate([to_all(moved, ("x", "z")), share.reshape(4 * n_z, -1, batch)], axis=1)
    first, weight, later = lax.optimization_barrier((first, weight, cotangent))
    first = exchange(first, ("x", "z"))

    arrived = [lax.ppermute(later, ("ylo", "yhi"), SPREAD[j]) for j in range(4)]
    far, arrived = lax.optimization_barrier((far, arrived))
    own_core, other_core = (weight, far), (trade(weight, "core"), trade(far, "core"))
    arrived = jnp.stack(arrived)
    first, own_core, other_core, arrived = lax.optimization_barrier((first, own_core, other_core, arrived))
    summed = add_up(first[:, batch:])
    beside = trade(summed, "ylo")
    panels = first[:, :batch].reshape(2, 2, n_z, batch, block)
    panels = [
        lax.dynamic_index_in_dim(panels, c, 1, keepdims=False).transpose(0, 2, 1, 3).reshape(2 * batch, depth)
        for c in (core, 1 - core)
    ]
    frozen = [
        (dot(panels[0], own_core[i], ((1,), (0,))) + dot(panels[1], other_core[i], ((1,), (0,)))).astype(BF16)
        for i in range(2)
    ]
    frozen = jnp.stack([f.reshape(2, batch, hidden) for f in frozen], axis=1).reshape(4, batch, hidden)
    kept = [lax.dynamic_index_in_dim(arrived, high ^ ylo ^ p, 0, keepdims=False) for p in (0, 2, 1, 3)]
    column = jnp.concatenate([*kept[:2], trade(jnp.concatenate(kept[2:]), "ylo")])
    frozen = sum(
        lax.ppermute(
            lax.dynamic_index_in_dim(frozen, high ^ j ^ ylo, 0, keepdims=False), ("ylo", "yhi"), HOME[j]
        ).astype(F32)
        for j in range(4)
    )

    slabs = slabs_of(core, high ^ ylo, own_core, other_core, arrived, summed.shape[0])
    slabs, beside = lax.optimization_barrier((slabs, beside))
    summed = (summed + beside).astype(BF16)
    second = exchange(
        lax.dynamic_update_slice(slabs, to_all(summed, ("x", "z")), (0, block, 0)), ("x", "z")
    )
    second, frozen = lax.optimization_barrier((second, frozen))
    gradient = lax.ppermute(add_up(second[:, :block]), ("x", "ylo", "yhi"), BACK)
    whole = second[:, block:].reshape(share.shape)
    low, along, back_low = whole[:rank], whole[rank : rank + past], whole[rank + past :]

    projection_output = (frozen + dot(low, up, ((0,), (0,)))).astype(BF16)
    token_input_gradient = (gradient + dot(down, back_low, ((1,), (0,)))).T.astype(BF16)

    kept = tokens.astype(F32).T - dot(directions, along, ((1,), (0,)))
    kept_high = kept.astype(BF16)
    kept_rest = (kept - kept_high.astype(F32)).astype(BF16)
    down_part = dot(back_low, kept_high, ((1,), (1,))) + dot(back_low, kept_rest, ((1,), (1,)))
    pair = exchange(to_all(jnp.concatenate([low, down_part.astype(BF16)], axis=0), "yhi"), "yhi")
    pair, column = lax.optimization_barrier((pair, column))
    lows = pair[:, :rank].reshape(2, 2, rank, batch)
    lows = [lax.dynamic_index_in_dim(lows, l, 1, keepdims=False) for l in (ylo, 1 - ylo)]
    up_part = dot(jnp.concatenate([*lows[0], *lows[1]], axis=1), column, ((1,), (0,)))
    ours = jnp.concatenate([up_part, add_up(pair[:, rank:])], axis=1)
    ours = ours + trade(ours.astype(BF16), "core").astype(F32)
    grad_up, grad_down = ours[:, :hidden], ours[:, hidden:].T
    return projection_output, token_input_gradient, grad_down, grad_up


def solution(mesh):
    fine = Mesh(mesh.devices.reshape(SIZES), AXES)
    placed = (P(DP, SHARD), P(DP, SHARD), P(SHARD, None), P(None, SHARD), P(DP, SHARD), P(SHARD, None))
    return jax.shard_map(
        local,
        mesh=fine,
        in_specs=placed,
        out_specs=(P(DP, SHARD), P(DP, SHARD), P(SHARD, None), P(None, SHARD)),
        check_vma=False,
    )
```

```python
import jax
import jax.numpy as jnp
from jax import lax
from jax.experimental import pallas as pl
from jax.experimental.pallas import tpu as pltpu
from jax.sharding import Mesh
from jax.sharding import PartitionSpec as P

F32 = jnp.float32
BF16 = jnp.bfloat16
AXES = ("x", "ylo", "z", "yhi", "core")
SIZES = (4, 2, 8, 4, 2)
SHARD = ("x", "ylo", "z")
DP = ("yhi", "core")
THERE = [
    ((x * 2 + l) * 4 + h, ((2 * (h // 2) + l) * 2 + h % 2) * 4 + x)
    for x in range(4)
    for l in range(2)
    for h in range(4)
]
BACK = [(b, a) for a, b in THERE]
HOME = [
    [(l * 4 + h, ((h ^ j) % 2) * 4 + (h ^ j) // 2 * 2 + l) for l in range(2) for h in range(4)] for j in range(4)
]


SPREAD = [
    [(l * 4 + h, (h % 2) * 4 + ((h // 2 * 2 + l) ^ j)) for l in range(2) for h in range(4)] for j in range(4)
]


def dot(left, right, contract):
    return lax.dot_general(left, right, ((contract[0], contract[1]), ((), ())), preferred_element_type=F32)


def exchange(pieces, axes):
    return lax.all_to_all(pieces, axes, split_axis=0, concat_axis=0, tiled=True)


def to_all(block, axes):
    return jnp.broadcast_to(block[None], (lax.axis_size(axes), *block.shape))


def add_up(pieces):
    return jnp.sum(pieces.astype(F32), axis=0)


def trade(block, axis):
    return lax.ppermute(block, axis, [(0, 1), (1, 0)])


def slab_kernel(where_ref, near_ref, far_ref, near_beside_ref, far_beside_ref, arrived_ref, out_ref):
    first = where_ref[1]
    block = batch = out_ref.shape[4]

    def write(own_weight, other_weight):
        total = None
        for l, weight in enumerate((own_weight, other_weight)):
            right = jnp.concatenate([arrived_ref[first ^ l], arrived_ref[first ^ l ^ 2]], axis=0)
            part = lax.dot_general(weight, right, (((1,), (1,)), ((), ())), preferred_element_type=F32)
            total = part if total is None else total + part
        total = total.astype(BF16)
        for i in range(2):
            for j in range(out_ref.shape[2]):
                out_ref[i, 0, j, :block, :] = total[j * block : (j + 1) * block, i * batch : (i + 1) * batch]

    @pl.when(pl.program_id(0) == 0)
    def _():
        write(near_ref[...], far_ref[...])

    @pl.when(pl.program_id(0) == 1)
    def _():
        write(near_beside_ref[...], far_beside_ref[...])


def slabs_of(core, first, own_core, other_core, arrived, extra):
    batch = arrived.shape[1]
    block, take = batch, 8
    depth, hidden = own_core[0].shape
    steps = depth // (take * block)
    early = pl.BlockSpec((take * block, hidden), lambda s, r, _: (jnp.where(s == 0, r, steps - 1), 0))
    late = pl.BlockSpec((take * block, hidden), lambda s, r, _: (jnp.where(s == 0, 0, r), 0))
    whole = pl.BlockSpec(arrived.shape, lambda s, r, _: (0, 0, 0))
    out = pl.pallas_call(
        slab_kernel,
        grid_spec=pltpu.PrefetchScalarGridSpec(
            num_scalar_prefetch=1,
            grid=(2, steps),
            in_specs=[early, early, late, late, whole],
            out_specs=pl.BlockSpec(
                (2, 1, take, block + extra, batch), lambda s, r, c: (0, s ^ c[0], r, 0, 0)
            ),
        ),
        out_shape=jax.ShapeDtypeStruct((2, 2, steps * take, block + extra, batch), BF16),
        cost_estimate=pl.CostEstimate(
            flops=16 * depth * hidden * batch, bytes_accessed=8 * depth * hidden, transcendentals=0
        ),
    )(jnp.stack([core, first]), *own_core, *other_core, arrived)
    return out.reshape(4 * steps * take, block + extra, batch)


def local(tokens, weight, down, up, cotangent, directions):
    n_z = lax.axis_size("z")
    batch, block = tokens.shape
    rank = down.shape[1]
    past = directions.shape[1]
    depth, hidden = weight.shape

    ylo, high, core = (lax.axis_index(a) for a in ("ylo", "yhi", "core"))
    moved = lax.ppermute(tokens, ("x", "ylo", "yhi"), THERE)
    moved, weight = lax.optimization_barrier((moved, weight))
    far = trade(weight, "ylo")

    share = jnp.concatenate(
        [
            dot(down, tokens, ((0,), (1,))),
            dot(directions, tokens, ((0,), (1,))),
            dot(up, cotangent, ((1,), (1,))),
        ],
        axis=0,
    ).astype(BF16)
    first = jnp.concatenate([to_all(moved, ("x", "z")), share.reshape(4 * n_z, -1, batch)], axis=1)
    first, weight, later = lax.optimization_barrier((first, weight, cotangent))
    first = exchange(first, ("x", "z"))

    arrived = [lax.ppermute(later, ("ylo", "yhi"), SPREAD[j]) for j in range(4)]
    far, arrived = lax.optimization_barrier((far, arrived))
    own_core, other_core = (weight, far), (trade(weight, "core"), trade(far, "core"))
    arrived = jnp.stack(arrived)
    first, own_core, other_core, arrived = lax.optimization_barrier((first, own_core, other_core, arrived))
    summed = add_up(first[:, batch:])
    beside = trade(summed, "ylo")
    panels = first[:, :batch].reshape(2, 2, n_z, batch, block)
    panels = [
        lax.dynamic_index_in_dim(panels, c, 1, keepdims=False).transpose(0, 2, 1, 3).reshape(2 * batch, depth)
        for c in (core, 1 - core)
    ]
    frozen = [
        (dot(panels[0], own_core[i], ((1,), (0,))) + dot(panels[1], other_core[i], ((1,), (0,)))).astype(BF16)
        for i in range(2)
    ]
    frozen = jnp.stack([f.reshape(2, batch, hidden) for f in frozen], axis=1).reshape(4, batch, hidden)
    kept = [lax.dynamic_index_in_dim(arrived, high ^ ylo ^ p, 0, keepdims=False) for p in (0, 2, 1, 3)]
    column = jnp.concatenate([*kept[:2], trade(jnp.concatenate(kept[2:]), "ylo")])
    frozen, column = lax.optimization_barrier((frozen, column))
    frozen = sum(
        lax.ppermute(
            lax.dynamic_index_in_dim(frozen, high ^ j ^ ylo, 0, keepdims=False), ("ylo", "yhi"), HOME[j]
        ).astype(F32)
        for j in range(4)
    )

    slabs = slabs_of(core, high ^ ylo, own_core, other_core, arrived, summed.shape[0])
    slabs, beside = lax.optimization_barrier((slabs, beside))
    summed = (summed + beside).astype(BF16)
    second = exchange(
        lax.dynamic_update_slice(slabs, to_all(summed, ("x", "z")), (0, block, 0)), ("x", "z")
    )
    second, frozen = lax.optimization_barrier((second, frozen))
    gradient = lax.ppermute(add_up(second[:, :block]), ("x", "ylo", "yhi"), BACK)
    whole = second[:, block:].reshape(share.shape)
    low, along, back_low = whole[:rank], whole[rank : rank + past], whole[rank + past :]

    projection_output = (frozen + dot(low, up, ((0,), (0,)))).astype(BF16)
    token_input_gradient = (gradient + dot(down, back_low, ((1,), (0,)))).T.astype(BF16)

    kept = tokens.astype(F32).T - dot(directions, along, ((1,), (0,)))
    kept_high = kept.astype(BF16)
    kept_rest = (kept - kept_high.astype(F32)).astype(BF16)
    down_part = dot(back_low, kept_high, ((1,), (1,))) + dot(back_low, kept_rest, ((1,), (1,)))
    pair = exchange(to_all(jnp.concatenate([low, down_part.astype(BF16)], axis=0), "yhi"), "yhi")
    lows = pair[:, :rank].reshape(2, 2, rank, batch)
    lows = [lax.dynamic_index_in_dim(lows, l, 1, keepdims=False) for l in (ylo, 1 - ylo)]
    up_part = dot(jnp.concatenate([*lows[0], *lows[1]], axis=1), column, ((1,), (0,)))
    ours = jnp.concatenate([up_part, add_up(pair[:, rank:])], axis=1)
    ours = ours + trade(ours.astype(BF16), "core").astype(F32)
    grad_up, grad_down = ours[:, :hidden], ours[:, hidden:].T
    return projection_output, token_input_gradient, grad_down, grad_up


def solution(mesh):
    fine = Mesh(mesh.devices.reshape(SIZES), AXES)
    placed = (P(DP, SHARD), P(DP, SHARD), P(SHARD, None), P(None, SHARD), P(DP, SHARD), P(SHARD, None))
    return jax.shard_map(
        local,
        mesh=fine,
        in_specs=placed,
        out_specs=(P(DP, SHARD), P(DP, SHARD), P(SHARD, None), P(None, SHARD)),
        check_vma=False,
    )
```
